32 devices in a mesh: freq: 4 (over z), mic: 8 (over y, x, core).
Axes of the slice: x: 2, y: 2, z: 4, core: 2. Of those that a mesh axis runs over, the one named last changes fastest.
Arguments:
- spectra: float32 [8, 2048, 1024], P('freq', 'mic'), parts along dimension 0, may hold values from -50 to 50
- mic_pos: float32 [3, 2048], replicated, may hold values from -1 to 1
- focus_pts: float32 [3, 1024], replicated, may hold values from -1 to 1
- wavenumber: float32 [4], P('freq'), parts along dimension 0, may hold values from 20 to 120
Outputs:
- csm: float32 [8, 2048, 2048], P('freq', 'mic'), parts along dimension 0
- beam: float32 [4096], P(('freq', 'mic')), parts along dimension 0
The draws below stay inside these ranges and needn't reach their ends.
There are 4 independent parts, one for each index of `freq`. The reference program is written for one: setup_inputs(seed, part) draws one part's arguments, and reference() takes and returns one part's arrays. A program takes and returns all parts, laid end to end along the dimension named above; an argument that names none is the same for every part. Nothing has to cross between parts.
All inputs are finite; a program needn't handle non-finite values.
Results may differ from the reference program's by a relative error of at most 0.0003.
Values sent between devices are 32-bit elements; how exact they have to be, the bound alone decides.
A program may use at most 128 MiB of HBM per device.

```python
import math
import jax
import jax.numpy as jnp
from jax import lax

MICS = 2048
SNAPSHOTS = 1024
FOCUS = 1024


def draw_spectra(key, part):
    keys = jax.random.split(key, 5)
    index = jnp.arange(MICS).astype(jnp.float32)
    ramp = 1.0 + 2.0 * index / MICS
    level = jax.random.uniform(keys[0], (MICS,), jnp.float32, 0.5, 2.0)
    noise = jax.random.truncated_normal(keys[1], -4.0, 4.0, (2, MICS, SNAPSHOTS), jnp.float32) * 0.7071
    amplitude = jnp.sqrt(level * ramp)
    phases = jax.random.uniform(keys[2], (4, MICS, 1), jnp.float32, -3.14159, 3.14159)
    source_real = jax.random.truncated_normal(keys[3], -4.0, 4.0, (4, 1, SNAPSHOTS), jnp.float32) * 0.3536
    source_imag = jax.random.truncated_normal(keys[4], -4.0, 4.0, (4, 1, SNAPSHOTS), jnp.float32) * 0.3536
    cosine = jnp.cos(phases)
    sine = jnp.sin(phases)
    part_real = source_real * cosine - source_imag * sine
    part_imag = source_real * sine + source_imag * cosine
    signal_real = part_real[0] + part_real[1] + part_real[2] + part_real[3]
    signal_imag = part_imag[0] + part_imag[1] + part_imag[2] + part_imag[3]
    signal = jnp.stack([signal_real, signal_imag])
    return (signal + noise) * amplitude[None, :, None]


def setup_inputs(seed: int = 0, part: int = 0) -> dict:
    arg_keys = jax.random.split(jax.random.key(seed), 5)
    part_splits = jax.random.split(jax.random.fold_in(arg_keys[4], part), 5)
    return {
        "spectra": draw_spectra(jax.random.fold_in(jax.random.fold_in(arg_keys[4], part), 71), part),
        "mic_pos": jnp.clip(jax.random.uniform(arg_keys[1], (3, MICS), jnp.float32, -1.0, 1.0), -1.0, 1.0),
        "focus_pts": jnp.clip(jax.random.uniform(arg_keys[2], (3, FOCUS), jnp.float32, -1.0, 1.0), -1.0, 1.0),
        "wavenumber": jnp.clip(jnp.exp(jax.random.uniform(part_splits[3], (1,), jnp.float32, math.log(20.0), math.log(120.0))), 20.0, 120.0),
    }


standoff_sq = 2.25

def inner(left, right):
    return lax.dot_general(left, right, (((1,), (1,)), ((), ())), precision=lax.Precision.HIGHEST, preferred_element_type=jnp.float32)

def contract(left, right):
    return lax.dot_general(left, right, (((0,), (0,)), ((), ())), precision=lax.Precision.HIGHEST, preferred_element_type=jnp.float32)

def cross_block(rows, cols, count):
    real_part = (inner(rows[0], cols[0]) + inner(rows[1], cols[1])) / count
    imag_part = (inner(rows[1], cols[0]) - inner(rows[0], cols[1])) / count
    return jnp.stack([real_part, imag_part])

def steering(mic_pos, focus_pts, wave, count):
    diff = mic_pos[:, :, None] - focus_pts[:, None, :]
    dist = jnp.sqrt(diff[0] * diff[0] + diff[1] * diff[1] + diff[2] * diff[2] + standoff_sq)
    phase = wave * dist
    scale = 1.0 / math.sqrt(count)
    return (jnp.cos(phase) * scale, -jnp.sin(phase) * scale)

def reference(spectra, mic_pos, focus_pts, wavenumber):
    csm = cross_block(spectra, spectra, SNAPSHOTS)
    g_real, g_imag = steering(mic_pos, focus_pts, wavenumber[0], MICS)
    along_real = contract(g_real, spectra[0]) + contract(g_imag, spectra[1])
    along_imag = contract(g_real, spectra[1]) - contract(g_imag, spectra[0])
    power = lax.optimization_barrier(jnp.sum(along_real * along_real + along_imag * along_imag, axis=1)) / SNAPSHOTS
    diagonal = jnp.sum(spectra[0] * spectra[0] + spectra[1] * spectra[1]) / SNAPSHOTS
    beam = power - diagonal / MICS
    return (csm, beam)
```

```python
import functools
import math

import jax
import jax.numpy as jnp
from jax import lax
from jax.experimental import pallas as pl
from jax.experimental.pallas import tpu as pltpu
from jax.sharding import PartitionSpec as P

standoff_sq = 2.25
MESH = pl.DeviceIdType.MESH

SIN_COEF = (3.141592640144165, -5.167710084047848, 2.550077528428822, -0.598291299770303, 0.07765766117753167)
COS_COEF = (0.9999999532943689, -4.934792832496617, 4.058411371007551, -1.331876617475819, 0.21968961468319229)


def inner(left, right):
    return lax.dot_general(
        left,
        right,
        (((1,), (1,)), ((), ())),
        precision=lax.Precision.HIGH,
        preferred_element_type=jnp.float32,
    )


def contract(left, right):
    return lax.dot_general(
        left,
        right,
        (((0,), (0,)), ((), ())),
        precision=lax.Precision.HIGH,
        preferred_element_type=jnp.float32,
    )


def cross_block(rows, cols, count):
    real_part = (inner(rows[0], cols[0]) + inner(rows[1], cols[1])) / count
    imag_part = (inner(rows[1], cols[0]) - inner(rows[0], cols[1])) / count
    return jnp.stack([real_part, imag_part])


def steering(mic_pos, focus_pts, wave, count):
    diff = mic_pos[:, :, None] - focus_pts[:, None, :]
    dist = jnp.sqrt(diff[0] * diff[0] + diff[1] * diff[1] + diff[2] * diff[2] + standoff_sq)
    phase = wave * dist
    scale = 1.0 / math.sqrt(count)
    return (jnp.cos(phase) * scale, -jnp.sin(phase) * scale)


def general(spectra, mic_pos, focus_pts, wavenumber):
    count = spectra.shape[2]
    all_mics = mic_pos.shape[1]
    all_focus = focus_pts.shape[1]
    n_dev = lax.axis_size("mic")
    me_index = lax.axis_index("mic")
    wave = wavenumber[0]
    own_count = all_focus // n_dev
    own_focus = lax.dynamic_slice_in_dim(focus_pts, me_index * own_count, own_count, 1)
    piece = lax.all_gather(spectra, "mic", axis=1, tiled=True)
    block = cross_block(spectra, piece, count)
    g_real, g_imag = steering(mic_pos, own_focus, wave, all_mics)
    along_real = contract(g_real, piece[0]) + contract(g_imag, piece[1])
    along_imag = contract(g_real, piece[1]) - contract(g_imag, piece[0])
    squares = jnp.sum(piece[0] * piece[0] + piece[1] * piece[1])
    power = jnp.sum(along_real * along_real + along_imag * along_imag, axis=1) / count
    beam = power - squares / count / all_mics
    return (block, beam)


HALF = 128
BLOCK = 256


def dot_nt(left, right):
    return lax.dot_general(left, right, (((1,), (1,)), ((), ())), preferred_element_type=jnp.float32)


def dot_nn(left, right):
    return lax.dot_general(left, right, (((1,), (0,)), ((), ())), preferred_element_type=jnp.float32)


def dot3(dot, left, right):
    return dot(left[0], right[0]) + (dot(left[0], right[1]) + dot(left[1], right[0]))


def split(value):
    high = value.astype(jnp.bfloat16)
    low = (value - high.astype(jnp.float32)).astype(jnp.bfloat16)
    return high, low


def horner(coef, z):
    out = jnp.full_like(z, coef[-1])
    for c in coef[-2::-1]:
        out = out * z + c
    return out


def kernel(
    x_ref, mic_ref, foc_ref, wave_ref, c_ref, beam_ref,
    own, recv, xh, xl, gh, gl, cst, chl, dbuf, dhb, pacc, ptx, prx,
    loc_sem, out_sem, ss, rs, fs, fr, ds, dr, bs, br,
):
    count = x_ref.shape[2]
    all_mics = mic_ref.shape[1]
    all_focus = foc_ref.shape[1]
    me = lax.axis_index("mic")
    y, x, h = me // 4, (me // 2) % 2, me % 2

    def index(yy, xx, hh):
        return yy * 4 + xx * 2 + hh

    sib = index(y, x, 1 - h)
    xd, xo = index(y, 1 - x, h), index(y, 1 - x, 1 - h)
    yd, yo = index(1 - y, x, (h + y) % 2), index(1 - y, x, (h + y + 1) % 2)
    yt = index(1 - y, x, (h + 1 - y) % 2)

    barrier = pltpu.get_barrier_semaphore()
    for j in range(1, 8):
        pl.semaphore_signal(barrier, inc=1, device_id={"mic": (me + j) % 8}, device_id_type=MESH)
    pl.semaphore_wait(barrier, 7)

    def half(t):
        return pl.ds(pl.multiple_of(t * HALF, HALF), HALF)

    def main_copy(t, which):
        return pltpu.make_async_remote_copy(
            src_ref=x_ref.at[:, half(t), :],
            dst_ref=recv.at[1 + which, :, half(t), :],
            send_sem=ss.at[1 + 2 * t + which],
            recv_sem=rs.at[1 + 2 * t + which],
            device_id={"mic": yt if which else xd},
            device_id_type=MESH,
        )

    def forward(t, which):
        return pltpu.make_async_remote_copy(
            src_ref=recv.at[1 + which, :, half(t), :],
            dst_ref=recv.at[3 + which, :, half(t), :],
            send_sem=fs.at[2 * t + which],
            recv_sem=fr.at[2 * t + which],
            device_id={"mic": sib},
            device_id_type=MESH,
        )

    sib_copy = pltpu.make_async_remote_copy(
        src_ref=x_ref,
        dst_ref=recv.at[0],
        send_sem=ss.at[0],
        recv_sem=rs.at[0],
        device_id={"mic": sib},
        device_id_type=MESH,
    )

    def cols(dev, t):
        return pl.ds(pl.multiple_of(dev * BLOCK + t * HALF, HALF), HALF)

    def piece_copy(p, role):
        a, b = p // 2, p % 2
        if role == 0:
            src, rows, to = dbuf.at[p], half(a), xd
            where = cols(yd, b)
        else:
            src, rows, to = dhb.at[p], half(b), yd
            where = cols(xd, a)
        return pltpu.make_async_remote_copy(
            src_ref=src,
            dst_ref=c_ref.at[:, rows, where],
            send_sem=ds.at[2 * p + role],
            recv_sem=dr.at[2 * p + role],
            device_id={"mic": to},
            device_id_type=MESH,
        )

    def out_copy(v, dev, t, hf):
        return pltpu.make_async_copy(
            cst.at[v, :, :, hf * HALF : (hf + 1) * HALF],
            c_ref.at[:, :, cols(dev, t)],
            out_sem.at[2 * v + hf],
        )

    for t in range(2):
        main_copy(t, 0).start()
        main_copy(t, 1).start()
        if t == 0:
            sib_copy.start()
    own_copy = pltpu.make_async_copy(x_ref, own, loc_sem)
    own_copy.start()

    pacc[...] = jnp.zeros_like(pacc)

    turns = wave_ref[0] * (0.5 / math.pi)
    owners = [(me, me), (sib, sib), (xd, yd), (xo, yo), (xd, yd), (xo, yo)]

    def steer_half(v, hf):
        dev = owners[v][hf]
        t = hf if v < 2 else (v - 2) // 2
        at = cols(dev, t)
        mic = [
            jnp.transpose(jnp.broadcast_to(mic_ref[c : c + 1, at], (HALF, HALF))) for c in range(3)
        ]

        def tile(n, carry):
            lanes = pl.ds(pl.multiple_of(n * HALF, HALF), HALF)
            total = None
            for c in range(3):
                d = mic[c] - foc_ref[c : c + 1, lanes]
                total = d * d if total is None else total + d * d
            turn = turns * jnp.sqrt(total + standoff_sq)
            f = turn - jnp.round(turn)
            z = f * f
            s = f * horner(SIN_COEF, z)
            c = horner(COS_COEF, z)
            both = (1.0 - 2.0 * s * s, -2.0 * s * c)
            for k in range(2):
                high, low = split(both[k])
                gh[v, k, hf * HALF : (hf + 1) * HALF, lanes] = high
                gl[v, k, hf * HALF : (hf + 1) * HALF, lanes] = low
            return carry

        lax.fori_loop(0, all_focus // HALF, tile, 0)

    def split_rows(load, v, row, rows):
        step = 32

        def body(i, carry):
            for k in range(2):
                high, low = split(load(k, i * step, step))
                at = pl.ds(pl.multiple_of(row + i * step, step), step)
                xh[v, k, at, :] = high
                xl[v, k, at, :] = low
            return carry

        lax.fori_loop(0, rows // step, body, 0)

    def spectra_of(v, k, rows):
        return xh[v, k, rows, :], xl[v, k, rows, :]

    def cross(v_left, rows_left, v_right, rows_right):
        left = [spectra_of(v_left, k, rows_left) for k in range(2)]
        right = [spectra_of(v_right, k, rows_right) for k in range(2)]
        real = dot3(dot_nt, left[0], right[0]) + dot3(dot_nt, left[1], right[1])
        imag = dot3(dot_nt, left[1], right[0]) - dot3(dot_nt, left[0], right[1])
        return real * (1.0 / count), imag * (1.0 / count)

    whole = slice(0, BLOCK)
    first, second = slice(0, HALF), slice(HALF, BLOCK)

    def csm_block(v):
        real, imag = cross(0, whole, v, whole)
        cst[v, 0] = real
        cst[v, 1] = imag

    def power(m, left, right, weight):
        width = 256

        def tile(n, carry):
            lanes = pl.ds(pl.multiple_of(n * width, width), width)
            c = [(chl[0, k, :m, :], chl[1, k, :m, :]) for k in range(2)]
            g = [right(k, lanes) for k in range(2)]
            zr = dot3(dot_nn, c[0], g[0]) - dot3(dot_nn, c[1], g[1])
            zi = dot3(dot_nn, c[0], g[1]) + dot3(dot_nn, c[1], g[0])
            lr, li = left(0, lanes), left(1, lanes)
            p = lr * zr + li * zi
            p = jnp.sum(p.reshape(m // 8, 8, width), axis=0)
            pacc[:, lanes] += weight * p
            return carry

        lax.fori_loop(0, all_focus // width, tile, 0)

    def beam_block(v, drop_diagonal):
        for k in range(2):
            value = cst[v, k]
            if drop_diagonal is not None and k == 0:
                row = lax.broadcasted_iota(jnp.int32, (BLOCK, BLOCK), 0)
                col = lax.broadcasted_iota(jnp.int32, (BLOCK, BLOCK), 1)
                value = jnp.where((row == col) & drop_diagonal, 0.0, value)
            high, low = split(value)
            chl[0, k] = high
            chl[1, k] = low

        def left(k, lanes):
            return gh[0, k, :, lanes].astype(jnp.float32) + gl[0, k, :, lanes].astype(jnp.float32)

        def right(k, lanes):
            return gh[v, k, :, lanes], gl[v, k, :, lanes]

        power(BLOCK, left, right, 1.0)

    for v in range(2):
        for hf in range(2):
            steer_half(v, hf)
    own_copy.wait()
    split_rows(lambda k, r, n: own[k, pl.ds(pl.multiple_of(r, n), n), :], 0, 0, BLOCK)
    sib_copy.wait_recv()
    split_rows(lambda k, r, n: recv[0, k, pl.ds(pl.multiple_of(r, n), n), :], 1, 0, BLOCK)

    def near(v, carry):
        csm_block(v)
        beam_block(v, v == 0)
        return carry

    lax.fori_loop(0, 2, near, 0)
    for hf in range(2):
        out_copy(0, me, hf, hf).start()
        out_copy(1, sib, hf, hf).start()
    for v in range(2, 6):
        for hf in range(2):
            steer_half(v, hf)

    def phase(t, carry):
        def rows_of(slot):
            def load(k, r, n):
                return recv[slot, k, pl.ds(pl.multiple_of(t * HALF + r, n), n), :]
            return load

        for which in range(2):
            main_copy(t, which).wait_recv()
            forward(t, which).start()
        split_rows(rows_of(1), 2 + 2 * t, 0, HALF)
        split_rows(rows_of(2), 2 + 2 * t, HALF, HALF)

        def piece(p, inner_carry):
            real, imag = cross(2 + 2 * (p // 2), first, 2 + 2 * (p % 2), second)
            dbuf[p, 0] = real
            dbuf[p, 1] = imag
            piece_copy(p, 0).start()
            dhb[p, 0] = jnp.transpose(real)
            dhb[p, 1] = -jnp.transpose(imag)
            piece_copy(p, 1).start()
            return inner_carry

        lax.fori_loop(t, 1 + 3 * t, piece, 0)

        def far(o, inner_carry):
            v = 2 + 2 * t + o
            csm_block(v)
            beam_block(v, None)
            return inner_carry

        for which in range(2):
            forward(t, which).wait_recv()
        split_rows(rows_of(3), 3 + 2 * t, 0, HALF)
        split_rows(rows_of(4), 3 + 2 * t, HALF, HALF)
        lax.fori_loop(0, 2, far, 0)
        out_copy(2 + 2 * t, xd, t, 0).start()
        out_copy(2 + 2 * t, yd, t, 1).start()
        out_copy(3 + 2 * t, xo, t, 0).start()
        out_copy(3 + 2 * t, yo, t, 1).start()
        return carry

    lax.fori_loop(0, 2, phase, 0)

    def mirrored(a, carry):
        for k in range(2):
            for b in range(2):
                high, low = split(dbuf[2 * a + b, k])
                chl[0, k, :HALF, b * HALF : (b + 1) * HALF] = high
                chl[1, k, :HALF, b * HALF : (b + 1) * HALF] = low

        def left(k, lanes):
            v = 2 + 2 * a
            return gh[v, k, first, lanes].astype(jnp.float32) + gl[v, k, first, lanes].astype(jnp.float32)

        def right(k, lanes):
            return tuple(
                jnp.concatenate([g[2, k, second, lanes], g[4, k, second, lanes]], axis=0)
                for g in (gh, gl)
            )

        power(HALF, left, right, 2.0)
        return carry

    lax.fori_loop(0, 2, mirrored, 0)

    for j in range(8):
        ptx[j] = jnp.sum(pacc[:, j * HALF : (j + 1) * HALF], axis=0, keepdims=True) * (1.0 / all_mics)

    def beam_copy(j):
        to = (me + j) % 8
        return pltpu.make_async_remote_copy(
            src_ref=ptx.at[to],
            dst_ref=prx.at[j],
            send_sem=bs.at[j],
            recv_sem=br.at[j],
            device_id={"mic": to},
            device_id_type=MESH,
        )

    for j in range(1, 8):
        beam_copy(j).start()
    total = ptx[me]
    for j in range(1, 8):
        beam_copy(j).wait_recv()
        total = total + prx[j]
    beam_ref[...] = total

    for j in range(1, 8):
        beam_copy(j).wait_send()
    sib_copy.wait_send()
    for t in range(2):
        for which in range(2):
            main_copy(t, which).wait_send()
            forward(t, which).wait_send()
    for hf in range(2):
        out_copy(0, me, hf, hf).wait()
        out_copy(1, sib, hf, hf).wait()
    for t in range(2):
        out_copy(2 + 2 * t, xd, t, 0).wait()
        out_copy(2 + 2 * t, yd, t, 1).wait()
        out_copy(3 + 2 * t, xo, t, 0).wait()
        out_copy(3 + 2 * t, yo, t, 1).wait()
    for p in range(4):
        for role in range(2):
            piece_copy(p, role).wait_send()
            piece_copy(p, role).wait_recv()


def exchange(spectra, mic_pos, focus_pts, wavenumber):
    rows, count = spectra.shape[1:]
    all_mics = mic_pos.shape[1]
    all_focus = focus_pts.shape[1]
    f32, bf16 = jnp.float32, jnp.bfloat16
    dma = pltpu.SemaphoreType.DMA
    csm, beam = pl.pallas_call(
        kernel,
        out_shape=(
            jax.ShapeDtypeStruct((2, rows, all_mics), f32),
            jax.ShapeDtypeStruct((1, all_focus // 8), f32),
        ),
        in_specs=[
            pl.BlockSpec(memory_space=pl.ANY),
            pl.BlockSpec(memory_space=pltpu.VMEM),
            pl.BlockSpec(memory_space=pltpu.VMEM),
            pl.BlockSpec(memory_space=pltpu.SMEM),
        ],
        out_specs=(pl.BlockSpec(memory_space=pl.ANY), pl.BlockSpec(memory_space=pltpu.VMEM)),
        scratch_shapes=[
            pltpu.VMEM((2, rows, count), f32),
            pltpu.VMEM((5, 2, rows, count), f32),
            pltpu.VMEM((6, 2, rows, count), bf16),
            pltpu.VMEM((6, 2, rows, count), bf16),
            pltpu.VMEM((6, 2, rows, all_focus), bf16),
            pltpu.VMEM((6, 2, rows, all_focus), bf16),
            pltpu.VMEM((6, 2, rows, rows), f32),
            pltpu.VMEM((2, 2, rows, rows), bf16),
            pltpu.VMEM((4, 2, HALF, HALF), f32),
            pltpu.VMEM((4, 2, HALF, HALF), f32),
            pltpu.VMEM((8, all_focus), f32),
            pltpu.VMEM((8, 1, HALF), f32),
            pltpu.VMEM((8, 1, HALF), f32),
            dma(()),
            dma((12,)),
            dma((5,)),
            dma((5,)),
            dma((4,)),
            dma((4,)),
            dma((8,)),
            dma((8,)),
            dma((8,)),
            dma((8,)),
        ],
        compiler_params=pltpu.CompilerParams(
            collective_id=0, has_side_effects=True, vmem_limit_bytes=58 * 1024 * 1024
        ),
    )(spectra, mic_pos, focus_pts, wavenumber)
    return csm, beam.reshape(all_focus // 8)


def solution(mesh):
    def per_device(spectra, mic_pos, focus_pts, wavenumber):
        fits = (
            mesh.shape["mic"] == 8
            and spectra.shape[1] == BLOCK
            and spectra.shape[2] % HALF == 0
            and focus_pts.shape[1] == 8 * HALF
        )
        body = exchange if fits else general
        return body(spectra, mic_pos, focus_pts, wavenumber)

    in_specs = (P("freq", "mic", None), P(), P(), P("freq"))
    out_specs = (P("freq", "mic", None), P(("freq", "mic")))
    return jax.shard_map(
        per_device, mesh=mesh, in_specs=in_specs, out_specs=out_specs, check_vma=False
    )
```

```python
import functools
import math

import jax
import jax.numpy as jnp
from jax import lax
from jax.experimental import pallas as pl
from jax.experimental.pallas import tpu as pltpu
from jax.sharding import PartitionSpec as P

standoff_sq = 2.25
MESH = pl.DeviceIdType.MESH

SIN_COEF = (3.141592640144165, -5.167710084047848, 2.550077528428822, -0.598291299770303, 0.07765766117753167)
COS_COEF = (0.9999999532943689, -4.934792832496617, 4.058411371007551, -1.331876617475819, 0.21968961468319229)


def inner(left, right):
    return lax.dot_general(
        left,
        right,
        (((1,), (1,)), ((), ())),
        precision=lax.Precision.HIGH,
        preferred_element_type=jnp.float32,
    )


def contract(left, right):
    return lax.dot_general(
        left,
        right,
        (((0,), (0,)), ((), ())),
        precision=lax.Precision.HIGH,
        preferred_element_type=jnp.float32,
    )


def cross_block(rows, cols, count):
    real_part = (inner(rows[0], cols[0]) + inner(rows[1], cols[1])) / count
    imag_part = (inner(rows[1], cols[0]) - inner(rows[0], cols[1])) / count
    return jnp.stack([real_part, imag_part])


def steering(mic_pos, focus_pts, wave, count):
    diff = mic_pos[:, :, None] - focus_pts[:, None, :]
    dist = jnp.sqrt(diff[0] * diff[0] + diff[1] * diff[1] + diff[2] * diff[2] + standoff_sq)
    phase = wave * dist
    scale = 1.0 / math.sqrt(count)
    return (jnp.cos(phase) * scale, -jnp.sin(phase) * scale)


def general(spectra, mic_pos, focus_pts, wavenumber):
    count = spectra.shape[2]
    all_mics = mic_pos.shape[1]
    all_focus = focus_pts.shape[1]
    n_dev = lax.axis_size("mic")
    me_index = lax.axis_index("mic")
    wave = wavenumber[0]
    own_count = all_focus // n_dev
    own_focus = lax.dynamic_slice_in_dim(focus_pts, me_index * own_count, own_count, 1)
    piece = lax.all_gather(spectra, "mic", axis=1, tiled=True)
    block = cross_block(spectra, piece, count)
    g_real, g_imag = steering(mic_pos, own_focus, wave, all_mics)
    along_real = contract(g_real, piece[0]) + contract(g_imag, piece[1])
    along_imag = contract(g_real, piece[1]) - contract(g_imag, piece[0])
    squares = jnp.sum(piece[0] * piece[0] + piece[1] * piece[1])
    power = jnp.sum(along_real * along_real + along_imag * along_imag, axis=1) / count
    beam = power - squares / count / all_mics
    return (block, beam)


HALF = 128
BLOCK = 256


def dot_nt(left, right):
    return lax.dot_general(left, right, (((1,), (1,)), ((), ())), preferred_element_type=jnp.float32)


def dot_nn(left, right):
    return lax.dot_general(left, right, (((1,), (0,)), ((), ())), preferred_element_type=jnp.float32)


def dot3(dot, left, right):
    return dot(left[0], right[0]) + (dot(left[0], right[1]) + dot(left[1], right[0]))


def split(value):
    high = value.astype(jnp.bfloat16)
    low = (value - high.astype(jnp.float32)).astype(jnp.bfloat16)
    return high, low


def horner(coef, z):
    out = jnp.full_like(z, coef[-1])
    for c in coef[-2::-1]:
        out = out * z + c
    return out


def kernel(
    x_ref, mic_ref, foc_ref, wave_ref, c_ref, beam_ref,
    own, recv, xh, xl, gh, gl, cst, chl, dbuf, dhb, pacc, ptx, prx,
    loc_sem, out_sem, ss, rs, fs, fr, ds, dr, bs, br,
):
    count = x_ref.shape[2]
    all_mics = mic_ref.shape[1]
    all_focus = foc_ref.shape[1]
    me = lax.axis_index("mic")
    y, x, h = me // 4, (me // 2) % 2, me % 2

    def index(yy, xx, hh):
        return yy * 4 + xx * 2 + hh

    sib = index(y, x, 1 - h)
    xd, xo = index(y, 1 - x, h), index(y, 1 - x, 1 - h)
    yd, yo = index(1 - y, x, (h + y) % 2), index(1 - y, x, (h + y + 1) % 2)
    yt = index(1 - y, x, (h + 1 - y) % 2)

    barrier = pltpu.get_barrier_semaphore()
    for j in range(1, 8):
        pl.semaphore_signal(barrier, inc=1, device_id={"mic": (me + j) % 8}, device_id_type=MESH)
    pl.semaphore_wait(barrier, 7)

    def half(t):
        return pl.ds(pl.multiple_of(t * HALF, HALF), HALF)

    def main_copy(t, which):
        return pltpu.make_async_remote_copy(
            src_ref=x_ref.at[:, half(t), :],
            dst_ref=recv.at[1 + which, :, half(t), :],
            send_sem=ss.at[1 + 2 * t + which],
            recv_sem=rs.at[1 + 2 * t + which],
            device_id={"mic": yt if which else xd},
            device_id_type=MESH,
        )

    def forward(t, which):
        return pltpu.make_async_remote_copy(
            src_ref=recv.at[1 + which, :, half(t), :],
            dst_ref=recv.at[3 + which, :, half(t), :],
            send_sem=fs.at[2 * t + which],
            recv_sem=fr.at[2 * t + which],
            device_id={"mic": sib},
            device_id_type=MESH,
        )

    sib_copy = pltpu.make_async_remote_copy(
        src_ref=x_ref,
        dst_ref=recv.at[0],
        send_sem=ss.at[0],
        recv_sem=rs.at[0],
        device_id={"mic": sib},
        device_id_type=MESH,
    )

    def cols(dev, t):
        return pl.ds(pl.multiple_of(dev * BLOCK + t * HALF, HALF), HALF)

    def piece_copy(p, role):
        a, b = p // 2, p % 2
        if role == 0:
            src, rows, to = dbuf.at[p], half(a), xd
            where = cols(yd, b)
        else:
            src, rows, to = dhb.at[p], half(b), yd
            where = cols(xd, a)
        return pltpu.make_async_remote_copy(
            src_ref=src,
            dst_ref=c_ref.at[:, rows, where],
            send_sem=ds.at[2 * p + role],
            recv_sem=dr.at[2 * p + role],
            device_id={"mic": to},
            device_id_type=MESH,
        )

    def out_copy(v, dev, t, hf):
        return pltpu.make_async_copy(
            cst.at[v, :, :, hf * HALF : (hf + 1) * HALF],
            c_ref.at[:, :, cols(dev, t)],
            out_sem.at[2 * v + hf],
        )

    for t in range(2):
        main_copy(t, 0).start()
        main_copy(t, 1).start()
        if t == 0:
            sib_copy.start()
    own_copy = pltpu.make_async_copy(x_ref, own, loc_sem)
    own_copy.start()

    pacc[...] = jnp.zeros_like(pacc)

    turns = wave_ref[0] * (0.5 / math.pi)
    owners = [(me, me), (sib, sib), (xd, yd), (xo, yo), (xd, yd), (xo, yo)]

    def steer_half(v, hf):
        dev = owners[v][hf]
        t = hf if v < 2 else (v - 2) // 2
        at = cols(dev, t)
        mic = [
            jnp.transpose(jnp.broadcast_to(mic_ref[c : c + 1, at], (HALF, HALF))) for c in range(3)
        ]

        def tile(n, carry):
            lanes = pl.ds(pl.multiple_of(n * HALF, HALF), HALF)
            total = None
            for c in range(3):
                d = mic[c] - foc_ref[c : c + 1, lanes]
                total = d * d if total is None else total + d * d
            turn = turns * jnp.sqrt(total + standoff_sq)
            f = turn - jnp.round(turn)
            z = f * f
            s = f * horner(SIN_COEF, z)
            c = horner(COS_COEF, z)
            both = (1.0 - 2.0 * s * s, -2.0 * s * c)
            for k in range(2):
                high, low = split(both[k])
                gh[v, k, hf * HALF : (hf + 1) * HALF, lanes] = high
                gl[v, k, hf * HALF : (hf + 1) * HALF, lanes] = low
            return carry

        lax.fori_loop(0, all_focus // HALF, tile, 0)

    def split_rows(load, v, row, rows):
        step = 32

        def body(i, carry):
            for k in range(2):
                high, low = split(load(k, i * step, step))
                at = pl.ds(pl.multiple_of(row + i * step, step), step)
                xh[v, k, at, :] = high
                xl[v, k, at, :] = low
            return carry

        lax.fori_loop(0, rows // step, body, 0)

    def spectra_of(v, k, rows):
        return xh[v, k, rows, :], xl[v, k, rows, :]

    def cross(v_left, rows_left, v_right, rows_right):
        left = [spectra_of(v_left, k, rows_left) for k in range(2)]
        right = [spectra_of(v_right, k, rows_right) for k in range(2)]
        real = dot3(dot_nt, left[0], right[0]) + dot3(dot_nt, left[1], right[1])
        imag = dot3(dot_nt, left[1], right[0]) - dot3(dot_nt, left[0], right[1])
        return real * (1.0 / count), imag * (1.0 / count)

    whole = slice(0, BLOCK)
    first, second = slice(0, HALF), slice(HALF, BLOCK)

    def csm_block(v):
        real, imag = cross(0, whole, v, whole)
        cst[v, 0] = real
        cst[v, 1] = imag

    def power(m, left, right, weight):
        width = 256

        def tile(n, carry):
            lanes = pl.ds(pl.multiple_of(n * width, width), width)
            c = [(chl[0, k, :m, :], chl[1, k, :m, :]) for k in range(2)]
            g = [right(k, lanes) for k in range(2)]
            zr = dot3(dot_nn, c[0], g[0]) - dot3(dot_nn, c[1], g[1])
            zi = dot3(dot_nn, c[0], g[1]) + dot3(dot_nn, c[1], g[0])
            lr, li = left(0, lanes), left(1, lanes)
            p = lr * zr + li * zi
            p = jnp.sum(p.reshape(m // 8, 8, width), axis=0)
            pacc[:, lanes] += weight * p
            return carry

        lax.fori_loop(0, all_focus // width, tile, 0)

    def beam_block(v, drop_diagonal, row=0, late_weight=1.0):
        m = BLOCK - row
        for k in range(2):
            value = cst[v, k, row:, :]
            if drop_diagonal is not None and k == 0:
                r = lax.broadcasted_iota(jnp.int32, (BLOCK, BLOCK), 0)
                c = lax.broadcasted_iota(jnp.int32, (BLOCK, BLOCK), 1)
                value = jnp.where((r == c) & drop_diagonal, 0.0, value)
            high, low = split(value)
            chl[0, k, :m, :] = high
            chl[1, k, :m, :] = low

        def left(k, lanes):
            value = gh[0, k, row:, lanes].astype(jnp.float32) + gl[0, k, row:, lanes].astype(jnp.float32)
            if late_weight == 1.0:
                return value
            return jnp.concatenate([value[:HALF], late_weight * value[HALF:]], axis=0)

        def right(k, lanes):
            return gh[v, k, :, lanes], gl[v, k, :, lanes]

        power(m, left, right, 1.0)

    for v in range(2):
        for hf in range(2):
            steer_half(v, hf)
    own_copy.wait()
    split_rows(lambda k, r, n: own[k, pl.ds(pl.multiple_of(r, n), n), :], 0, 0, BLOCK)
    sib_copy.wait_recv()
    split_rows(lambda k, r, n: recv[0, k, pl.ds(pl.multiple_of(r, n), n), :], 1, 0, BLOCK)

    def near(v, carry):
        csm_block(v)
        beam_block(v, v == 0)
        return carry

    lax.fori_loop(0, 2, near, 0)
    for hf in range(2):
        out_copy(0, me, hf, hf).start()
        out_copy(1, sib, hf, hf).start()
    for v in range(2, 6):
        for hf in range(2):
            steer_half(v, hf)

    def mirrored(a, carry):
        for k in range(2):
            for b in range(2):
                high, low = split(dbuf[2 * a + b, k])
                chl[0, k, :HALF, b * HALF : (b + 1) * HALF] = high
                chl[1, k, :HALF, b * HALF : (b + 1) * HALF] = low

        def left(k, lanes):
            v = 2 + 2 * a
            return gh[v, k, first, lanes].astype(jnp.float32) + gl[v, k, first, lanes].astype(jnp.float32)

        def right(k, lanes):
            return tuple(
                jnp.concatenate([g[2, k, second, lanes], g[4, k, second, lanes]], axis=0)
                for g in (gh, gl)
            )

        power(HALF, left, right, 2.0)
        return carry


    for t in range(2):
        def rows_of(slot):
            def load(k, r, n):
                return recv[slot, k, pl.ds(pl.multiple_of(t * HALF + r, n), n), :]
            return load

        def far(v, x_dev, y_dev):
            csm_block(v)
            out_copy(v, x_dev, t, 0).start()
            out_copy(v, y_dev, t, 1).start()
            if t == 0:
                beam_block(v, None, 0, 2.0)
            else:
                beam_block(v, None, HALF)

        def piece(p, carry):
            real, imag = cross(2 + 2 * (p // 2), first, 2 + 2 * (p % 2), second)
            dbuf[p, 0] = real
            dbuf[p, 1] = imag
            piece_copy(p, 0).start()
            dhb[p, 0] = jnp.transpose(real)
            dhb[p, 1] = -jnp.transpose(imag)
            piece_copy(p, 1).start()
            return carry

        for which in range(2):
            main_copy(t, which).wait_recv()
            forward(t, which).start()
        split_rows(rows_of(1), 2 + 2 * t, 0, HALF)
        split_rows(rows_of(2), 2 + 2 * t, HALF, HALF)
        lax.fori_loop(t, 1 + 3 * t, piece, 0)
        far(2 + 2 * t, xd, yd)
        for which in range(2):
            forward(t, which).wait_recv()
        split_rows(rows_of(3), 3 + 2 * t, 0, HALF)
        split_rows(rows_of(4), 3 + 2 * t, HALF, HALF)
        far(3 + 2 * t, xo, yo)

    lax.fori_loop(0, 2, mirrored, 0)

    for j in range(8):
        ptx[j] = jnp.sum(pacc[:, j * HALF : (j + 1) * HALF], axis=0, keepdims=True) * (1.0 / all_mics)

    def beam_copy(j):
        to = (me + j) % 8
        return pltpu.make_async_remote_copy(
            src_ref=ptx.at[to],
            dst_ref=prx.at[j],
            send_sem=bs.at[j],
            recv_sem=br.at[j],
            device_id={"mic": to},
            device_id_type=MESH,
        )

    for j in range(1, 8):
        beam_copy(j).start()
    total = ptx[me]
    for j in range(1, 8):
        beam_copy(j).wait_recv()
        total = total + prx[j]
    beam_ref[...] = total

    for j in range(1, 8):
        beam_copy(j).wait_send()
    sib_copy.wait_send()
    for t in range(2):
        for which in range(2):
            main_copy(t, which).wait_send()
            forward(t, which).wait_send()
    for hf in range(2):
        out_copy(0, me, hf, hf).wait()
        out_copy(1, sib, hf, hf).wait()
    for t in range(2):
        out_copy(2 + 2 * t, xd, t, 0).wait()
        out_copy(2 + 2 * t, yd, t, 1).wait()
        out_copy(3 + 2 * t, xo, t, 0).wait()
        out_copy(3 + 2 * t, yo, t, 1).wait()
    for p in range(4):
        for role in range(2):
            piece_copy(p, role).wait_send()
            piece_copy(p, role).wait_recv()


def exchange(spectra, mic_pos, focus_pts, wavenumber):
    rows, count = spectra.shape[1:]
    all_mics = mic_pos.shape[1]
    all_focus = focus_pts.shape[1]
    f32, bf16 = jnp.float32, jnp.bfloat16
    dma = pltpu.SemaphoreType.DMA
    csm, beam = pl.pallas_call(
        kernel,
        out_shape=(
            pltpu.VMEM((2, rows, all_mics), f32),
            jax.ShapeDtypeStruct((1, all_focus // 8), f32),
        ),
        in_specs=[
            pl.BlockSpec(memory_space=pl.ANY),
            pl.BlockSpec(memory_space=pltpu.VMEM),
            pl.BlockSpec(memory_space=pltpu.VMEM),
            pl.BlockSpec(memory_space=pltpu.SMEM),
        ],
        out_specs=(pl.BlockSpec(memory_space=pltpu.VMEM), pl.BlockSpec(memory_space=pltpu.VMEM)),
        scratch_shapes=[
            pltpu.VMEM((2, rows, count), f32),
            pltpu.VMEM((5, 2, rows, count), f32),
            pltpu.VMEM((6, 2, rows, count), bf16),
            pltpu.VMEM((6, 2, rows, count), bf16),
            pltpu.VMEM((6, 2, rows, all_focus), bf16),
            pltpu.VMEM((6, 2, rows, all_focus), bf16),
            pltpu.VMEM((6, 2, rows, rows), f32),
            pltpu.VMEM((2, 2, rows, rows), bf16),
            pltpu.VMEM((4, 2, HALF, HALF), f32),
            pltpu.VMEM((4, 2, HALF, HALF), f32),
            pltpu.VMEM((8, all_focus), f32),
            pltpu.VMEM((8, 1, HALF), f32),
            pltpu.VMEM((8, 1, HALF), f32),
            dma(()),
            dma((12,)),
            dma((5,)),
            dma((5,)),
            dma((4,)),
            dma((4,)),
            dma((8,)),
            dma((8,)),
            dma((8,)),
            dma((8,)),
        ],
        compiler_params=pltpu.CompilerParams(
            collective_id=0, has_side_effects=True, vmem_limit_bytes=54 * 1024 * 1024
        ),
    )(spectra, mic_pos, focus_pts, wavenumber)
    return csm, beam.reshape(all_focus // 8)


def solution(mesh):
    def per_device(spectra, mic_pos, focus_pts, wavenumber):
        fits = (
            mesh.shape["mic"] == 8
            and spectra.shape[1] == BLOCK
            and spectra.shape[2] % HALF == 0
            and focus_pts.shape[1] == 8 * HALF
        )
        body = exchange if fits else general
        return body(spectra, mic_pos, focus_pts, wavenumber)

    in_specs = (P("freq", "mic", None), P(), P(), P("freq"))
    out_specs = (P("freq", "mic", None), P(("freq", "mic")))
    return jax.shard_map(
        per_device, mesh=mesh, in_specs=in_specs, out_specs=out_specs, check_vma=False
    )
```

```python
import functools
import math

import jax
import jax.numpy as jnp
from jax import lax
from jax.experimental import pallas as pl
from jax.experimental.pallas import tpu as pltpu
from jax.sharding import PartitionSpec as P

standoff_sq = 2.25
MESH = pl.DeviceIdType.MESH

SIN_COEF = (3.141592640144165, -5.167710084047848, 2.550077528428822, -0.598291299770303, 0.07765766117753167)
COS_COEF = (0.9999999532943689, -4.934792832496617, 4.058411371007551, -1.331876617475819, 0.21968961468319229)


def inner(left, right):
    return lax.dot_general(
        left,
        right,
        (((1,), (1,)), ((), ())),
        precision=lax.Precision.HIGH,
        preferred_element_type=jnp.float32,
    )


def contract(left, right):
    return lax.dot_general(
        left,
        right,
        (((0,), (0,)), ((), ())),
        precision=lax.Precision.HIGH,
        preferred_element_type=jnp.float32,
    )


def cross_block(rows, cols, count):
    real_part = (inner(rows[0], cols[0]) + inner(rows[1], cols[1])) / count
    imag_part = (inner(rows[1], cols[0]) - inner(rows[0], cols[1])) / count
    return jnp.stack([real_part, imag_part])


def steering(mic_pos, focus_pts, wave, count):
    diff = mic_pos[:, :, None] - focus_pts[:, None, :]
    dist = jnp.sqrt(diff[0] * diff[0] + diff[1] * diff[1] + diff[2] * diff[2] + standoff_sq)
    phase = wave * dist
    scale = 1.0 / math.sqrt(count)
    return (jnp.cos(phase) * scale, -jnp.sin(phase) * scale)


def general(spectra, mic_pos, focus_pts, wavenumber):
    count = spectra.shape[2]
    all_mics = mic_pos.shape[1]
    all_focus = focus_pts.shape[1]
    n_dev = lax.axis_size("mic")
    me_index = lax.axis_index("mic")
    wave = wavenumber[0]
    own_count = all_focus // n_dev
    own_focus = lax.dynamic_slice_in_dim(focus_pts, me_index * own_count, own_count, 1)
    piece = lax.all_gather(spectra, "mic", axis=1, tiled=True)
    block = cross_block(spectra, piece, count)
    g_real, g_imag = steering(mic_pos, own_focus, wave, all_mics)
    along_real = contract(g_real, piece[0]) + contract(g_imag, piece[1])
    along_imag = contract(g_real, piece[1]) - contract(g_imag, piece[0])
    squares = jnp.sum(piece[0] * piece[0] + piece[1] * piece[1])
    power = jnp.sum(along_real * along_real + along_imag * along_imag, axis=1) / count
    beam = power - squares / count / all_mics
    return (block, beam)


HALF = 128
BLOCK = 256


def dot_nt(left, right):
    return lax.dot_general(left, right, (((1,), (1,)), ((), ())), preferred_element_type=jnp.float32)


def dot_nn(left, right):
    return lax.dot_general(left, right, (((1,), (0,)), ((), ())), preferred_element_type=jnp.float32)


def dot3(dot, left, right):
    return dot(left[0], right[0]) + (dot(left[0], right[1]) + dot(left[1], right[0]))


def split(value):
    high = value.astype(jnp.bfloat16)
    low = (value - high.astype(jnp.float32)).astype(jnp.bfloat16)
    return high, low


def horner(coef, z):
    out = jnp.full_like(z, coef[-1])
    for c in coef[-2::-1]:
        out = out * z + c
    return out


def kernel(
    x_ref, mic_ref, foc_ref, wave_ref, c_ref, beam_ref,
    own, recv, xh, xl, gh, gl, cst, chl, dbuf, dhb, pacc, ptx, prx,
    loc_sem, out_sem, ss, rs, fs, fr, ds, dr, bs, br,
):
    count = x_ref.shape[2]
    all_mics = mic_ref.shape[1]
    all_focus = foc_ref.shape[1]
    me = lax.axis_index("mic")
    y, x, h = me // 4, (me // 2) % 2, me % 2

    def index(yy, xx, hh):
        return yy * 4 + xx * 2 + hh

    sib = index(y, x, 1 - h)
    xd, xo = index(y, 1 - x, h), index(y, 1 - x, 1 - h)
    yd, yo = index(1 - y, x, (h + y) % 2), index(1 - y, x, (h + y + 1) % 2)
    yt = index(1 - y, x, (h + 1 - y) % 2)

    barrier = pltpu.get_barrier_semaphore()
    for j in range(1, 8):
        pl.semaphore_signal(barrier, inc=1, device_id={"mic": (me + j) % 8}, device_id_type=MESH)
    pl.semaphore_wait(barrier, 7)

    def half(t):
        return pl.ds(pl.multiple_of(t * HALF, HALF), HALF)

    def main_copy(t, which):
        return pltpu.make_async_remote_copy(
            src_ref=x_ref.at[:, half(t), :],
            dst_ref=recv.at[1 + which, :, half(t), :],
            send_sem=ss.at[1 + 2 * t + which],
            recv_sem=rs.at[1 + 2 * t + which],
            device_id={"mic": yt if which else xd},
            device_id_type=MESH,
        )

    def forward(t, which):
        return pltpu.make_async_remote_copy(
            src_ref=recv.at[1 + which, :, half(t), :],
            dst_ref=recv.at[3 + which, :, half(t), :],
            send_sem=fs.at[2 * t + which],
            recv_sem=fr.at[2 * t + which],
            device_id={"mic": sib},
            device_id_type=MESH,
        )

    sib_copy = pltpu.make_async_remote_copy(
        src_ref=x_ref,
        dst_ref=recv.at[0],
        send_sem=ss.at[0],
        recv_sem=rs.at[0],
        device_id={"mic": sib},
        device_id_type=MESH,
    )

    def cols(dev, t):
        return pl.ds(pl.multiple_of(dev * BLOCK + t * HALF, HALF), HALF)

    def piece_copy(p, role):
        a, b = p // 2, p % 2
        if role == 0:
            src, rows, to = dbuf.at[p], half(a), xd
            where = cols(yd, b)
        else:
            src, rows, to = dhb.at[p], half(b), yd
            where = cols(xd, a)
        return pltpu.make_async_remote_copy(
            src_ref=src,
            dst_ref=c_ref.at[:, rows, where],
            send_sem=ds.at[2 * p + role],
            recv_sem=dr.at[2 * p + role],
            device_id={"mic": to},
            device_id_type=MESH,
        )

    def out_copy(v, dev, t, hf):
        return pltpu.make_async_copy(
            cst.at[v, :, :, hf * HALF : (hf + 1) * HALF],
            c_ref.at[:, :, cols(dev, t)],
            out_sem.at[2 * v + hf],
        )

    for t in range(2):
        main_copy(t, 0).start()
        main_copy(t, 1).start()
    sib_copy.start()
    own_copy = pltpu.make_async_copy(x_ref, own, loc_sem)
    own_copy.start()

    pacc[...] = jnp.zeros_like(pacc)

    turns = wave_ref[0] * (0.5 / math.pi)
    owners = [(me, me), (sib, sib), (xd, yd), (xo, yo), (xd, yd), (xo, yo)]

    def steer_half(v, hf):
        dev = owners[v][hf]
        t = hf if v < 2 else (v - 2) // 2
        at = cols(dev, t)
        mic = [
            jnp.transpose(jnp.broadcast_to(mic_ref[c : c + 1, at], (HALF, HALF))) for c in range(3)
        ]

        def tile(n, carry):
            lanes = pl.ds(pl.multiple_of(n * HALF, HALF), HALF)
            total = None
            for c in range(3):
                d = mic[c] - foc_ref[c : c + 1, lanes]
                total = d * d if total is None else total + d * d
            turn = turns * jnp.sqrt(total + standoff_sq)
            f = turn - jnp.round(turn)
            z = f * f
            s = f * horner(SIN_COEF, z)
            c = horner(COS_COEF, z)
            both = (1.0 - 2.0 * s * s, -2.0 * s * c)
            for k in range(2):
                high, low = split(both[k])
                gh[v, k, hf * HALF : (hf + 1) * HALF, lanes] = high
                gl[v, k, hf * HALF : (hf + 1) * HALF, lanes] = low
            return carry

        lax.fori_loop(0, all_focus // HALF, tile, 0)

    def split_rows(load, v, row, rows):
        step = 32

        def body(i, carry):
            for k in range(2):
                high, low = split(load(k, i * step, step))
                at = pl.ds(pl.multiple_of(row + i * step, step), step)
                xh[v, k, at, :] = high
                xl[v, k, at, :] = low
            return carry

        lax.fori_loop(0, rows // step, body, 0)

    def spectra_of(v, k, rows):
        return xh[v, k, rows, :], xl[v, k, rows, :]

    def cross(v_left, rows_left, v_right, rows_right):
        left = [spectra_of(v_left, k, rows_left) for k in range(2)]
        right = [spectra_of(v_right, k, rows_right) for k in range(2)]
        real = dot3(dot_nt, left[0], right[0]) + dot3(dot_nt, left[1], right[1])
        imag = dot3(dot_nt, left[1], right[0]) - dot3(dot_nt, left[0], right[1])
        return real * (1.0 / count), imag * (1.0 / count)

    whole = slice(0, BLOCK)
    first, second = slice(0, HALF), slice(HALF, BLOCK)

    def csm_block(v):
        real, imag = cross(0, whole, v, whole)
        cst[v, 0] = real
        cst[v, 1] = imag

    def power(m, left, right, weight):
        width = 256

        def tile(n, carry):
            lanes = pl.ds(pl.multiple_of(n * width, width), width)
            c = [(chl[0, k, :m, :], chl[1, k, :m, :]) for k in range(2)]
            g = [right(k, lanes) for k in range(2)]
            zr = dot3(dot_nn, c[0], g[0]) - dot3(dot_nn, c[1], g[1])
            zi = dot3(dot_nn, c[0], g[1]) + dot3(dot_nn, c[1], g[0])
            lr, li = left(0, lanes), left(1, lanes)
            p = lr * zr + li * zi
            p = jnp.sum(p.reshape(m // 8, 8, width), axis=0)
            pacc[:, lanes] += weight * p
            return carry

        lax.fori_loop(0, all_focus // width, tile, 0)

    def beam_block(v, drop_diagonal, row=0, late_weight=1.0):
        m = BLOCK - row
        for k in range(2):
            value = cst[v, k, row:, :]
            if drop_diagonal is not None and k == 0:
                r = lax.broadcasted_iota(jnp.int32, (BLOCK, BLOCK), 0)
                c = lax.broadcasted_iota(jnp.int32, (BLOCK, BLOCK), 1)
                value = jnp.where((r == c) & drop_diagonal, 0.0, value)
            high, low = split(value)
            chl[0, k, :m, :] = high
            chl[1, k, :m, :] = low

        def left(k, lanes):
            value = gh[0, k, row:, lanes].astype(jnp.float32) + gl[0, k, row:, lanes].astype(jnp.float32)
            if late_weight == 1.0:
                return value
            return jnp.concatenate([value[:HALF], late_weight * value[HALF:]], axis=0)

        def right(k, lanes):
            return gh[v, k, :, lanes], gl[v, k, :, lanes]

        power(m, left, right, 1.0)

    for v in range(2):
        for hf in range(2):
            steer_half(v, hf)
    own_copy.wait()
    split_rows(lambda k, r, n: own[k, pl.ds(pl.multiple_of(r, n), n), :], 0, 0, BLOCK)
    sib_copy.wait_recv()
    split_rows(lambda k, r, n: recv[0, k, pl.ds(pl.multiple_of(r, n), n), :], 1, 0, BLOCK)

    def near(v, carry):
        csm_block(v)
        beam_block(v, v == 0)
        return carry

    lax.fori_loop(0, 2, near, 0)
    for hf in range(2):
        out_copy(0, me, hf, hf).start()
        out_copy(1, sib, hf, hf).start()
    for v in range(2, 6):
        for hf in range(2):
            steer_half(v, hf)

    def mirrored(a, carry):
        for k in range(2):
            for b in range(2):
                high, low = split(dbuf[2 * a + b, k])
                chl[0, k, :HALF, b * HALF : (b + 1) * HALF] = high
                chl[1, k, :HALF, b * HALF : (b + 1) * HALF] = low

        def left(k, lanes):
            v = 2 + 2 * a
            return gh[v, k, first, lanes].astype(jnp.float32) + gl[v, k, first, lanes].astype(jnp.float32)

        def right(k, lanes):
            return tuple(
                jnp.concatenate([g[2, k, second, lanes], g[4, k, second, lanes]], axis=0)
                for g in (gh, gl)
            )

        power(HALF, left, right, 2.0)
        return carry


    for t in range(2):
        def rows_of(slot):
            def load(k, r, n):
                return recv[slot, k, pl.ds(pl.multiple_of(t * HALF + r, n), n), :]
            return load

        def far(v, x_dev, y_dev):
            csm_block(v)
            out_copy(v, x_dev, t, 0).start()
            out_copy(v, y_dev, t, 1).start()
            if t == 0:
                beam_block(v, None, 0, 2.0)
            else:
                beam_block(v, None, HALF)

        def piece(p, carry):
            real, imag = cross(2 + 2 * (p // 2), first, 2 + 2 * (p % 2), second)
            dbuf[p, 0] = real
            dbuf[p, 1] = imag
            piece_copy(p, 0).start()
            dhb[p, 0] = jnp.transpose(real)
            dhb[p, 1] = -jnp.transpose(imag)
            piece_copy(p, 1).start()
            return carry

        for which in range(2):
            main_copy(t, which).wait_recv()
            forward(t, which).start()
        split_rows(rows_of(1), 2 + 2 * t, 0, HALF)
        split_rows(rows_of(2), 2 + 2 * t, HALF, HALF)
        lax.fori_loop(t, 1 + 3 * t, piece, 0)
        far(2 + 2 * t, xd, yd)
        for which in range(2):
            forward(t, which).wait_recv()
        split_rows(rows_of(3), 3 + 2 * t, 0, HALF)
        split_rows(rows_of(4), 3 + 2 * t, HALF, HALF)
        far(3 + 2 * t, xo, yo)

    lax.fori_loop(0, 2, mirrored, 0)

    for j in range(8):
        ptx[j] = jnp.sum(pacc[:, j * HALF : (j + 1) * HALF], axis=0, keepdims=True) * (1.0 / all_mics)

    def beam_copy(j):
        to = (me + j) % 8
        return pltpu.make_async_remote_copy(
            src_ref=ptx.at[to],
            dst_ref=prx.at[j],
            send_sem=bs.at[j],
            recv_sem=br.at[j],
            device_id={"mic": to},
            device_id_type=MESH,
        )

    for j in range(1, 8):
        beam_copy(j).start()
    total = ptx[me]
    for j in range(1, 8):
        beam_copy(j).wait_recv()
        total = total + prx[j]
    beam_ref[...] = total

    for j in range(1, 8):
        beam_copy(j).wait_send()
    sib_copy.wait_send()
    for t in range(2):
        for which in range(2):
            main_copy(t, which).wait_send()
            forward(t, which).wait_send()
    for hf in range(2):
        out_copy(0, me, hf, hf).wait()
        out_copy(1, sib, hf, hf).wait()
    for t in range(2):
        out_copy(2 + 2 * t, xd, t, 0).wait()
        out_copy(2 + 2 * t, yd, t, 1).wait()
        out_copy(3 + 2 * t, xo, t, 0).wait()
        out_copy(3 + 2 * t, yo, t, 1).wait()
    for p in range(4):
        for role in range(2):
            piece_copy(p, role).wait_send()
            piece_copy(p, role).wait_recv()


def exchange(spectra, mic_pos, focus_pts, wavenumber):
    rows, count = spectra.shape[1:]
    all_mics = mic_pos.shape[1]
    all_focus = focus_pts.shape[1]
    f32, bf16 = jnp.float32, jnp.bfloat16
    dma = pltpu.SemaphoreType.DMA
    csm, beam = pl.pallas_call(
        kernel,
        out_shape=(
            pltpu.VMEM((2, rows, all_mics), f32),
            jax.ShapeDtypeStruct((1, all_focus // 8), f32),
        ),
        in_specs=[
            pl.BlockSpec(memory_space=pl.ANY),
            pl.BlockSpec(memory_space=pltpu.VMEM),
            pl.BlockSpec(memory_space=pltpu.VMEM),
            pl.BlockSpec(memory_space=pltpu.SMEM),
        ],
        out_specs=(pl.BlockSpec(memory_space=pltpu.VMEM), pl.BlockSpec(memory_space=pltpu.VMEM)),
        scratch_shapes=[
            pltpu.VMEM((2, rows, count), f32),
            pltpu.VMEM((5, 2, rows, count), f32),
            pltpu.VMEM((6, 2, rows, count), bf16),
            pltpu.VMEM((6, 2, rows, count), bf16),
            pltpu.VMEM((6, 2, rows, all_focus), bf16),
            pltpu.VMEM((6, 2, rows, all_focus), bf16),
            pltpu.VMEM((6, 2, rows, rows), f32),
            pltpu.VMEM((2, 2, rows, rows), bf16),
            pltpu.VMEM((4, 2, HALF, HALF), f32),
            pltpu.VMEM((4, 2, HALF, HALF), f32),
            pltpu.VMEM((8, all_focus), f32),
            pltpu.VMEM((8, 1, HALF), f32),
            pltpu.VMEM((8, 1, HALF), f32),
            dma(()),
            dma((12,)),
            dma((5,)),
            dma((5,)),
            dma((4,)),
            dma((4,)),
            dma((8,)),
            dma((8,)),
            dma((8,)),
            dma((8,)),
        ],
        compiler_params=pltpu.CompilerParams(
            collective_id=0, has_side_effects=True, vmem_limit_bytes=54 * 1024 * 1024
        ),
    )(spectra, mic_pos, focus_pts, wavenumber)
    return csm, beam.reshape(all_focus // 8)


def solution(mesh):
    def per_device(spectra, mic_pos, focus_pts, wavenumber):
        fits = (
            mesh.shape["mic"] == 8
            and spectra.shape[1] == BLOCK
            and spectra.shape[2] % HALF == 0
            and focus_pts.shape[1] == 8 * HALF
        )
        body = exchange if fits else general
        return body(spectra, mic_pos, focus_pts, wavenumber)

    in_specs = (P("freq", "mic", None), P(), P(), P("freq"))
    out_specs = (P("freq", "mic", None), P(("freq", "mic")))
    return jax.shard_map(
        per_device, mesh=mesh, in_specs=in_specs, out_specs=out_specs, check_vma=False
    )
```

```python
import functools
import math

import jax
import jax.numpy as jnp
from jax import lax
from jax.experimental import pallas as pl
from jax.experimental.pallas import tpu as pltpu
from jax.sharding import PartitionSpec as P

standoff_sq = 2.25
MESH = pl.DeviceIdType.MESH

SIN_COEF = (3.141592640144165, -5.167710084047848, 2.550077528428822, -0.598291299770303, 0.07765766117753167)
COS_COEF = (0.9999999532943689, -4.934792832496617, 4.058411371007551, -1.331876617475819, 0.21968961468319229)


def inner(left, right):
    return lax.dot_general(
        left,
        right,
        (((1,), (1,)), ((), ())),
        precision=lax.Precision.HIGH,
        preferred_element_type=jnp.float32,
    )


def contract(left, right):
    return lax.dot_general(
        left,
        right,
        (((0,), (0,)), ((), ())),
        precision=lax.Precision.HIGH,
        preferred_element_type=jnp.float32,
    )


def cross_block(rows, cols, count):
    real_part = (inner(rows[0], cols[0]) + inner(rows[1], cols[1])) / count
    imag_part = (inner(rows[1], cols[0]) - inner(rows[0], cols[1])) / count
    return jnp.stack([real_part, imag_part])


def steering(mic_pos, focus_pts, wave, count):
    diff = mic_pos[:, :, None] - focus_pts[:, None, :]
    dist = jnp.sqrt(diff[0] * diff[0] + diff[1] * diff[1] + diff[2] * diff[2] + standoff_sq)
    phase = wave * dist
    scale = 1.0 / math.sqrt(count)
    return (jnp.cos(phase) * scale, -jnp.sin(phase) * scale)


def general(spectra, mic_pos, focus_pts, wavenumber):
    count = spectra.shape[2]
    all_mics = mic_pos.shape[1]
    all_focus = focus_pts.shape[1]
    n_dev = lax.axis_size("mic")
    me_index = lax.axis_index("mic")
    wave = wavenumber[0]
    own_count = all_focus // n_dev
    own_focus = lax.dynamic_slice_in_dim(focus_pts, me_index * own_count, own_count, 1)
    piece = lax.all_gather(spectra, "mic", axis=1, tiled=True)
    block = cross_block(spectra, piece, count)
    g_real, g_imag = steering(mic_pos, own_focus, wave, all_mics)
    along_real = contract(g_real, piece[0]) + contract(g_imag, piece[1])
    along_imag = contract(g_real, piece[1]) - contract(g_imag, piece[0])
    squares = jnp.sum(piece[0] * piece[0] + piece[1] * piece[1])
    power = jnp.sum(along_real * along_real + along_imag * along_imag, axis=1) / count
    beam = power - squares / count / all_mics
    return (block, beam)


HALF = 128
BLOCK = 256


def dot_nt(left, right):
    return lax.dot_general(left, right, (((1,), (1,)), ((), ())), preferred_element_type=jnp.float32)


def dot_nn(left, right):
    return lax.dot_general(left, right, (((1,), (0,)), ((), ())), preferred_element_type=jnp.float32)


def dot3(dot, left, right):
    return dot(left[0], right[0]) + (dot(left[0], right[1]) + dot(left[1], right[0]))


def split(value):
    high = value.astype(jnp.bfloat16)
    low = (value - high.astype(jnp.float32)).astype(jnp.bfloat16)
    return high, low


def horner(coef, z):
    out = jnp.full_like(z, coef[-1])
    for c in coef[-2::-1]:
        out = out * z + c
    return out


def kernel(
    x_ref, mic_ref, foc_ref, wave_ref, c_ref, beam_ref,
    own, recv, xh, xl, gh, gl, cst, chl, dbuf, dhb, pacc, ptx, prx,
    loc_sem, out_sem, ss, rs, fs, fr, ds, dr, bs, br,
):
    count = x_ref.shape[2]
    all_mics = mic_ref.shape[1]
    all_focus = foc_ref.shape[1]
    me = lax.axis_index("mic")
    y, x, h = me // 4, (me // 2) % 2, me % 2

    def index(yy, xx, hh):
        return yy * 4 + xx * 2 + hh

    sib = index(y, x, 1 - h)
    xd, xo = index(y, 1 - x, h), index(y, 1 - x, 1 - h)
    yd, yo = index(1 - y, x, (h + y) % 2), index(1 - y, x, (h + y + 1) % 2)
    yt = index(1 - y, x, (h + 1 - y) % 2)

    barrier = pltpu.get_barrier_semaphore()
    for j in range(1, 8):
        pl.semaphore_signal(barrier, inc=1, device_id={"mic": (me + j) % 8}, device_id_type=MESH)
    pl.semaphore_wait(barrier, 7)

    def half(t):
        return pl.ds(pl.multiple_of(t * HALF, HALF), HALF)

    def main_copy(t, which):
        return pltpu.make_async_remote_copy(
            src_ref=x_ref.at[:, half(t), :],
            dst_ref=recv.at[1 + which, :, half(t), :],
            send_sem=ss.at[1 + 2 * t + which],
            recv_sem=rs.at[1 + 2 * t + which],
            device_id={"mic": yt if which else xd},
            device_id_type=MESH,
        )

    def forward(t, which):
        return pltpu.make_async_remote_copy(
            src_ref=recv.at[1 + which, :, half(t), :],
            dst_ref=recv.at[3 + which, :, half(t), :],
            send_sem=fs.at[2 * t + which],
            recv_sem=fr.at[2 * t + which],
            device_id={"mic": sib},
            device_id_type=MESH,
        )

    sib_copy = pltpu.make_async_remote_copy(
        src_ref=x_ref,
        dst_ref=recv.at[0],
        send_sem=ss.at[0],
        recv_sem=rs.at[0],
        device_id={"mic": sib},
        device_id_type=MESH,
    )

    def cols(dev, t):
        return pl.ds(pl.multiple_of(dev * BLOCK + t * HALF, HALF), HALF)

    def piece_copy(p, role):
        a, b = p // 2, p % 2
        if role == 0:
            src, rows, to = dbuf.at[p], half(a), xd
            where = cols(yd, b)
        else:
            src, rows, to = dhb.at[p], half(b), yd
            where = cols(xd, a)
        return pltpu.make_async_remote_copy(
            src_ref=src,
            dst_ref=c_ref.at[:, rows, where],
            send_sem=ds.at[2 * p + role],
            recv_sem=dr.at[2 * p + role],
            device_id={"mic": to},
            device_id_type=MESH,
        )

    def out_copy(v, dev, t, hf):
        return pltpu.make_async_copy(
            cst.at[v, :, :, hf * HALF : (hf + 1) * HALF],
            c_ref.at[:, :, cols(dev, t)],
            out_sem.at[2 * v + hf],
        )

    for t in range(2):
        main_copy(t, 0).start()
        main_copy(t, 1).start()
    sib_copy.start()
    own_copy = pltpu.make_async_copy(x_ref, own, loc_sem)
    own_copy.start()

    pacc[...] = jnp.zeros_like(pacc)

    turns = wave_ref[0] * (0.5 / math.pi)
    owners = [(me, me), (sib, sib), (xd, yd), (xo, yo), (xd, yd), (xo, yo)]

    def steer_half(v, hf):
        dev = owners[v][hf]
        t = hf if v < 2 else (v - 2) // 2
        at = cols(dev, t)
        mic = [
            jnp.transpose(jnp.broadcast_to(mic_ref[c : c + 1, at], (HALF, HALF))) for c in range(3)
        ]

        def tile(n, carry):
            lanes = pl.ds(pl.multiple_of(n * HALF, HALF), HALF)
            total = None
            for c in range(3):
                d = mic[c] - foc_ref[c : c + 1, lanes]
                total = d * d if total is None else total + d * d
            turn = turns * jnp.sqrt(total + standoff_sq)
            f = turn - jnp.round(turn)
            z = f * f
            s = f * horner(SIN_COEF, z)
            c = horner(COS_COEF, z)
            both = (1.0 - 2.0 * s * s, -2.0 * s * c)
            for k in range(2):
                high, low = split(both[k])
                gh[v, k, hf * HALF : (hf + 1) * HALF, lanes] = high
                gl[v, k, hf * HALF : (hf + 1) * HALF, lanes] = low
            return carry

        lax.fori_loop(0, all_focus // HALF, tile, 0)

    def split_rows(load, v, row, rows):
        step = 32

        def body(i, carry):
            for k in range(2):
                high, low = split(load(k, i * step, step))
                at = pl.ds(pl.multiple_of(row + i * step, step), step)
                xh[v, k, at, :] = high
                xl[v, k, at, :] = low
            return carry

        lax.fori_loop(0, rows // step, body, 0)

    def spectra_of(v, k, rows):
        return xh[v, k, rows, :], xl[v, k, rows, :]

    def cross(v_left, rows_left, v_right, rows_right):
        left = [spectra_of(v_left, k, rows_left) for k in range(2)]
        right = [spectra_of(v_right, k, rows_right) for k in range(2)]
        real = dot3(dot_nt, left[0], right[0]) + dot3(dot_nt, left[1], right[1])
        imag = dot3(dot_nt, left[1], right[0]) - dot3(dot_nt, left[0], right[1])
        return real * (1.0 / count), imag * (1.0 / count)

    whole = slice(0, BLOCK)
    first, second = slice(0, HALF), slice(HALF, BLOCK)

    def csm_block(v):
        real, imag = cross(0, whole, v, whole)
        cst[v, 0] = real
        cst[v, 1] = imag

    def power(m, left, right, weight):
        width = 256

        def tile(n, carry):
            lanes = pl.ds(pl.multiple_of(n * width, width), width)
            sums = []
            for k in range(2):
                high, low = right(k, lanes)
                a = dot_nn(chl[: 4 * m, :], high)
                b = dot_nn(chl[: 2 * m, :], low)
                sums.append([a[i * m : (i + 1) * m] + a[(2 + i) * m : (3 + i) * m] + b[i * m : (i + 1) * m] for i in range(2)])
            zr = sums[0][0] - sums[1][1]
            zi = sums[1][0] + sums[0][1]
            lr, li = left(0, lanes), left(1, lanes)
            p = lr * zr + li * zi
            p = jnp.sum(p.reshape(m // 8, 8, width), axis=0)
            pacc[:, lanes] += weight * p
            return carry

        lax.fori_loop(0, all_focus // width, tile, 0)

    def beam_block(v, drop_diagonal, row=0, late_weight=1.0):
        m = BLOCK - row
        for k in range(2):
            value = cst[v, k, row:, :]
            if drop_diagonal is not None and k == 0:
                r = lax.broadcasted_iota(jnp.int32, (BLOCK, BLOCK), 0)
                c = lax.broadcasted_iota(jnp.int32, (BLOCK, BLOCK), 1)
                value = jnp.where((r == c) & drop_diagonal, 0.0, value)
            high, low = split(value)
            chl[k * m : (k + 1) * m, :] = high
            chl[(2 + k) * m : (3 + k) * m, :] = low

        def left(k, lanes):
            value = gh[0, k, row:, lanes].astype(jnp.float32) + gl[0, k, row:, lanes].astype(jnp.float32)
            if late_weight == 1.0:
                return value
            return jnp.concatenate([value[:HALF], late_weight * value[HALF:]], axis=0)

        def right(k, lanes):
            return gh[v, k, :, lanes], gl[v, k, :, lanes]

        power(m, left, right, 1.0)

    for v in range(2):
        for hf in range(2):
            steer_half(v, hf)
    own_copy.wait()
    split_rows(lambda k, r, n: own[k, pl.ds(pl.multiple_of(r, n), n), :], 0, 0, BLOCK)
    sib_copy.wait_recv()
    split_rows(lambda k, r, n: recv[0, k, pl.ds(pl.multiple_of(r, n), n), :], 1, 0, BLOCK)

    def near(v, carry):
        csm_block(v)
        beam_block(v, v == 0)
        return carry

    lax.fori_loop(0, 2, near, 0)
    for hf in range(2):
        out_copy(0, me, hf, hf).start()
        out_copy(1, sib, hf, hf).start()
    for v in range(2, 6):
        for hf in range(2):
            steer_half(v, hf)

    def mirrored(a, carry):
        for k in range(2):
            for b in range(2):
                high, low = split(dbuf[2 * a + b, k])
                chl[k * HALF : (k + 1) * HALF, b * HALF : (b + 1) * HALF] = high
                chl[(2 + k) * HALF : (3 + k) * HALF, b * HALF : (b + 1) * HALF] = low

        def left(k, lanes):
            v = 2 + 2 * a
            return gh[v, k, first, lanes].astype(jnp.float32) + gl[v, k, first, lanes].astype(jnp.float32)

        def right(k, lanes):
            return tuple(
                jnp.concatenate([g[2, k, second, lanes], g[4, k, second, lanes]], axis=0)
                for g in (gh, gl)
            )

        power(HALF, left, right, 2.0)
        return carry


    for t in range(2):
        def rows_of(slot):
            def load(k, r, n):
                return recv[slot, k, pl.ds(pl.multiple_of(t * HALF + r, n), n), :]
            return load

        def far(v, x_dev, y_dev):
            csm_block(v)
            out_copy(v, x_dev, t, 0).start()
            out_copy(v, y_dev, t, 1).start()
            if t == 0:
                beam_block(v, None, 0, 2.0)
            else:
                beam_block(v, None, HALF)

        def piece(p, carry):
            real, imag = cross(2 + 2 * (p // 2), first, 2 + 2 * (p % 2), second)
            dbuf[p, 0] = real
            dbuf[p, 1] = imag
            piece_copy(p, 0).start()
            dhb[p, 0] = jnp.transpose(real)
            dhb[p, 1] = -jnp.transpose(imag)
            piece_copy(p, 1).start()
            return carry

        for which in range(2):
            main_copy(t, which).wait_recv()
            forward(t, which).start()
        split_rows(rows_of(1), 2 + 2 * t, 0, HALF)
        split_rows(rows_of(2), 2 + 2 * t, HALF, HALF)
        lax.fori_loop(t, 1 + 3 * t, piece, 0)
        far(2 + 2 * t, xd, yd)
        for which in range(2):
            forward(t, which).wait_recv()
        split_rows(rows_of(3), 3 + 2 * t, 0, HALF)
        split_rows(rows_of(4), 3 + 2 * t, HALF, HALF)
        far(3 + 2 * t, xo, yo)

    lax.fori_loop(0, 2, mirrored, 0)

    for j in range(8):
        ptx[j] = jnp.sum(pacc[:, j * HALF : (j + 1) * HALF], axis=0, keepdims=True) * (1.0 / all_mics)

    def beam_copy(j):
        to = (me + j) % 8
        return pltpu.make_async_remote_copy(
            src_ref=ptx.at[to],
            dst_ref=prx.at[j],
            send_sem=bs.at[j],
            recv_sem=br.at[j],
            device_id={"mic": to},
            device_id_type=MESH,
        )

    for j in range(1, 8):
        beam_copy(j).start()
    total = ptx[me]
    for j in range(1, 8):
        beam_copy(j).wait_recv()
        total = total + prx[j]
    beam_ref[...] = total

    for j in range(1, 8):
        beam_copy(j).wait_send()
    sib_copy.wait_send()
    for t in range(2):
        for which in range(2):
            main_copy(t, which).wait_send()
            forward(t, which).wait_send()
    for hf in range(2):
        out_copy(0, me, hf, hf).wait()
        out_copy(1, sib, hf, hf).wait()
    for t in range(2):
        out_copy(2 + 2 * t, xd, t, 0).wait()
        out_copy(2 + 2 * t, yd, t, 1).wait()
        out_copy(3 + 2 * t, xo, t, 0).wait()
        out_copy(3 + 2 * t, yo, t, 1).wait()
    for p in range(4):
        for role in range(2):
            piece_copy(p, role).wait_send()
            piece_copy(p, role).wait_recv()


def exchange(spectra, mic_pos, focus_pts, wavenumber):
    rows, count = spectra.shape[1:]
    all_mics = mic_pos.shape[1]
    all_focus = focus_pts.shape[1]
    f32, bf16 = jnp.float32, jnp.bfloat16
    dma = pltpu.SemaphoreType.DMA
    csm, beam = pl.pallas_call(
        kernel,
        out_shape=(
            pltpu.VMEM((2, rows, all_mics), f32),
            jax.ShapeDtypeStruct((1, all_focus // 8), f32),
        ),
        in_specs=[
            pl.BlockSpec(memory_space=pl.ANY),
            pl.BlockSpec(memory_space=pltpu.VMEM),
            pl.BlockSpec(memory_space=pltpu.VMEM),
            pl.BlockSpec(memory_space=pltpu.SMEM),
        ],
        out_specs=(pl.BlockSpec(memory_space=pltpu.VMEM), pl.BlockSpec(memory_space=pltpu.VMEM)),
        scratch_shapes=[
            pltpu.VMEM((2, rows, count), f32),
            pltpu.VMEM((5, 2, rows, count), f32),
            pltpu.VMEM((6, 2, rows, count), bf16),
            pltpu.VMEM((6, 2, rows, count), bf16),
            pltpu.VMEM((6, 2, rows, all_focus), bf16),
            pltpu.VMEM((6, 2, rows, all_focus), bf16),
            pltpu.VMEM((6, 2, rows, rows), f32),
            pltpu.VMEM((4 * rows, rows), bf16),
            pltpu.VMEM((4, 2, HALF, HALF), f32),
            pltpu.VMEM((4, 2, HALF, HALF), f32),
            pltpu.VMEM((8, all_focus), f32),
            pltpu.VMEM((8, 1, HALF), f32),
            pltpu.VMEM((8, 1, HALF), f32),
            dma(()),
            dma((12,)),
            dma((5,)),
            dma((5,)),
            dma((4,)),
            dma((4,)),
            dma((8,)),
            dma((8,)),
            dma((8,)),
            dma((8,)),
        ],
        compiler_params=pltpu.CompilerParams(
            collective_id=0, has_side_effects=True, vmem_limit_bytes=54 * 1024 * 1024
        ),
    )(spectra, mic_pos, focus_pts, wavenumber)
    return csm, beam.reshape(all_focus // 8)


def solution(mesh):
    def per_device(spectra, mic_pos, focus_pts, wavenumber):
        fits = (
            mesh.shape["mic"] == 8
            and spectra.shape[1] == BLOCK
            and spectra.shape[2] % HALF == 0
            and focus_pts.shape[1] == 8 * HALF
        )
        body = exchange if fits else general
        return body(spectra, mic_pos, focus_pts, wavenumber)

    in_specs = (P("freq", "mic", None), P(), P(), P("freq"))
    out_specs = (P("freq", "mic", None), P(("freq", "mic")))
    return jax.shard_map(
        per_device, mesh=mesh, in_specs=in_specs, out_specs=out_specs, check_vma=False
    )
```
